256 devices in a mesh: ctx: 64 (over z, x, core), tp: 4 (over y).
Axes of the slice: x: 4, y: 4, z: 8, core: 2. Of those that a mesh axis runs over, the one named last changes fastest.
Arguments:
- queries: bfloat16 [32768, 4096], P('ctx', 'tp'), may hold values from -21 to 21
- key_rows: bfloat16 [32768, 512], P('ctx', 'tp'), may hold values from -6 to 6
- value_rows: bfloat16 [32768, 512], P('ctx', 'tp'), may hold values from -6 to 6
- keep_rows: int32 [64, 64], P('ctx'), may hold values from 0 to 511
Outputs:
- attended: bfloat16 [32768, 4096], P(('ctx', 'tp'))
The draws below stay inside these ranges and needn't reach their ends.
All inputs are finite; a program needn't handle non-finite values.
Results may differ from the reference program's by a relative error of at most 0.0075.
Values may be sent and summed in bfloat16 or wider, within the bound.
No kernel may reach another device: no remote copies, remote signals or barrier semaphores. Data moves between devices by JAX's collectives and lax.ppermute only.
A program may use at most 64 MiB of HBM per device.

```python
import jax
import jax.numpy as jnp
from jax import lax

HD = 128
GROUP = 8
KEEP = 64
BLK = 512
KVH = 4
TOKENS = 32768
N_CTX = 64


def draw_key_rows(key, part):
    key = jax.random.fold_in(key, 3)
    result = jax.random.truncated_normal(key, -6.0, 6.0, (TOKENS, KVH * HD), jnp.float32)
    return result.astype(jnp.bfloat16)


def draw_queries(key, part):
    key = jax.random.fold_in(key, 5)
    result = jax.random.truncated_normal(key, -6.0, 6.0, (TOKENS, KVH * GROUP * HD), jnp.float32)
    return result.astype(jnp.bfloat16)


def set_ends(drawn, key, least, top_value):
    place = [jax.random.randint(jax.random.fold_in(key, axis), (), 0, length) for axis, length in enumerate(drawn.shape)]
    widest = drawn.shape.index(max(drawn.shape))
    beside = place[:widest] + [(place[widest] + 1) % drawn.shape[widest]] + place[widest + 1:]
    return drawn.at[tuple(place)].set(least).at[tuple(beside)].set(top_value)


def levels(own_key, extent, pieces, low, high):
    factor_of, own = 1.0, jax.random.fold_in(own_key, 6)
    for dim, blocks in pieces:
        draws = jnp.exp(jax.random.uniform(jax.random.fold_in(own, dim), (blocks,), jnp.float32, low / len(pieces), high / len(pieces)))
        factor_of = factor_of * jnp.repeat(draws, extent[dim] // blocks).reshape([-1 if axis == dim else 1 for axis in range(len(extent))])
    return factor_of


def noise(rng, shape, spread, reach, shards=(), held_as=jnp.bfloat16):
    array = jax.random.normal(rng, shape, jnp.float32) * spread
    if len(shards) > 0:
        array = levels(rng, shape, shards, -0.22, 0.18) * array
    return jnp.clip(array, min=-reach, max=reach).astype(held_as)


def setup_inputs(seed: int = 0) -> dict:
    streams_of = jax.random.split(jax.random.key(seed), 5)
    return {
        "queries": draw_queries(jax.random.fold_in(streams_of[4], 71), 0),
        "key_rows": draw_key_rows(jax.random.fold_in(streams_of[4], 71), 0),
        "value_rows": noise(streams_of[2], (TOKENS, KVH * HD), 1.0, 6.0, ((0, 64), (1, 4))),
        "keep_rows": set_ends(jax.random.randint(streams_of[3], (N_CTX, KEEP), 0, BLK), jax.random.fold_in(streams_of[3], 1), 0, BLK - 1).astype(jnp.int32),
    }


def reference(queries, key_rows, value_rows, keep_rows):
    host_count = N_CTX
    key_blocks = key_rows.reshape(host_count, BLK, KVH * HD).astype(jnp.float32)
    value_blocks = value_rows.reshape(host_count, BLK, KVH * HD).astype(jnp.float32)
    picker = (keep_rows[:, :, None] == jnp.arange(BLK, dtype=jnp.int32)[None, None, :]).astype(jnp.float32)
    passing_keys = jnp.einsum("hsb,hbc->hsc", picker, key_blocks).astype(jnp.bfloat16).reshape(host_count * KEEP, KVH, HD)
    passing_values = jnp.einsum("hsb,hbc->hsc", picker, value_blocks).astype(jnp.bfloat16).reshape(host_count * KEEP, KVH, HD)
    anchor_keys = key_rows[:BLK].reshape(BLK, KVH, HD)
    anchor_values = value_rows[:BLK].reshape(BLK, KVH, HD)
    passing_root = jnp.arange(host_count * KEEP, dtype=jnp.int32) // KEEP
    positions = jnp.arange(BLK, dtype=jnp.int32)

    def one_host(host):
        first_row = (host * BLK).astype(jnp.int32)
        query_block = lax.dynamic_slice_in_dim(queries, first_row, BLK, 0).reshape(BLK, KVH, GROUP, HD).astype(jnp.float32)
        own_keys = lax.dynamic_slice_in_dim(key_rows, first_row, BLK, 0).reshape(BLK, KVH, HD)
        own_values = lax.dynamic_slice_in_dim(value_rows, first_row, BLK, 0).reshape(BLK, KVH, HD)
        every_key = jnp.concatenate([anchor_keys, passing_keys, own_keys], axis=0).astype(jnp.float32)
        every_value = jnp.concatenate([anchor_values, passing_values, own_values], axis=0).astype(jnp.float32)
        visible = jnp.concatenate([
            jnp.broadcast_to(host >= 1, (BLK, BLK)),
            jnp.broadcast_to((passing_root < host)[None, :], (BLK, host_count * KEEP)),
            positions[None, :] <= positions[:, None]], axis=1)
        scores = jnp.einsum("qkgd,skd->kgqs", query_block, every_key) * (HD ** -0.5)
        scores = jnp.where(visible[None, None, :, :], scores, -jnp.inf)
        peak = jnp.max(scores, axis=-1, keepdims=True)
        exps = jnp.exp(scores - peak)
        totals = jnp.sum(exps, axis=-1)
        weights = exps.astype(jnp.bfloat16).astype(jnp.float32)
        summed = jnp.einsum("kgqs,skd->qkgd", weights, every_value)
        result = summed / jnp.transpose(totals, (2, 0, 1))[..., None]
        return result.reshape(BLK, KVH * GROUP * HD).astype(jnp.bfloat16)

    outputs = lax.map(one_host, jnp.arange(host_count, dtype=jnp.int32))
    return outputs.reshape(TOKENS, KVH * GROUP * HD)
```

```python
import functools

import jax
import jax.numpy as jnp
from jax import lax
from jax.experimental import pallas as pl
from jax.experimental.pallas import tpu as pltpu
from jax.sharding import PartitionSpec as P

BF = jnp.bfloat16
F32 = jnp.float32
Z, X, CORES = 8, 4, 2
HD, GROUP, KEEP, BLK = 128, 8, 64, 512
VROWS = HD + 16
DZ = (0, 1, -1, 2, -2, 3, -3, 4)
PAY = (len(DZ) + 1) * KEEP
LOG2E = 1.4426950408889634
SCALE = HD ** (-0.5) * LOG2E
LIMIT = 75.0 * 75.0 * HD
ROWS = 128
COLS = ROWS * GROUP
FINAL_HEADS = 8
VMEM = pl.BlockSpec(memory_space=pltpu.VMEM)
ANY = pl.BlockSpec(memory_space=pl.ANY)
NORM = jax.ShapeDtypeStruct((8, HD), F32)


def params():
    return pltpu.CompilerParams(vmem_limit_bytes=36 << 20)


def dot_t(a, b):
    return lax.dot_general(a, b, (((1,), (1,)), ((), ())), preferred_element_type=F32)


def dot(a, b):
    return lax.dot_general(a, b, (((1,), (0,)), ((), ())), preferred_element_type=F32)


def norm2(rows):
    rows = rows.astype(F32)
    most = jnp.max(jnp.sum(rows * rows, axis=1, keepdims=True), axis=0, keepdims=True)
    return jnp.broadcast_to(most, (8, HD))


def place():
    me = lax.axis_index("ctx")
    return me, me // (X * CORES), (me // CORES) % X, me % CORES


def origin_visible(dx, dcore, block):
    me, z, x, core = place()
    if block == len(DZ):
        return me >= 1
    host = ((z - DZ[block] + Z) % Z) * (X * CORES) + ((x - dx + X) % X) * CORES + (core + dcore) % CORES
    return host < me


def select_kernel(keep_ref, k_ref, v_ref, pass_ref, *piece_refs):
    chosen = (lax.broadcasted_iota(jnp.int32, (BLK, KEEP), 0) == keep_ref[...]).astype(BF)
    for side, ref in ((0, k_ref), (1, v_ref)):
        lanes = slice(side * HD, (side + 1) * HD)
        pass_ref[:, lanes] = lax.dot_general(
            chosen, ref[...], (((0,), (0,)), ((), ())), preferred_element_type=F32
        ).astype(BF)
        for x, piece_ref in enumerate(piece_refs):
            piece_ref[:, lanes] = ref[x * 2 * KEEP:(x + 1) * 2 * KEEP, :]


def same(shape):
    return pl.BlockSpec(shape, lambda *i: (0,) * len(shape))


def select(keep_rows, key_rows, value_rows):
    rows = [KEEP] + [2 * KEEP] * X
    return pl.pallas_call(
        select_kernel,
        grid=(1,),
        out_shape=tuple(jax.ShapeDtypeStruct((n, 2 * HD), BF) for n in rows),
        in_specs=[same((1, KEEP)), same((BLK, HD)), same((BLK, HD))],
        out_specs=tuple(same((n, 2 * HD)) for n in rows),
        compiler_params=params(),
        name="select",
    )(keep_rows, key_rows, value_rows)


def heads_below(q):
    return jnp.concatenate([q[:, h * HD:(h + 1) * HD] for h in range(q.shape[1] // HD)], axis=0)


def state_shape():
    return jax.ShapeDtypeStruct((BLK // ROWS, VROWS, COLS), F32)


STATE = pl.BlockSpec((1, VROWS, COLS), lambda i: (i, 0, 0))


def own_kernel(q_ref, k_ref, v_ref, state_ref, q_norm_ref, k_norm_ref, vt_ref):
    step = pl.program_id(0)

    @pl.when(step == 0)
    def _():
        vt_ref[:HD, :] = v_ref[...].astype(F32).T.astype(BF)
        rows = lax.broadcasted_iota(jnp.int32, (16, BLK), 0)
        vt_ref[HD:, :] = jnp.where(rows == 0, 1.0, 0.0).astype(BF)
        q_norm_ref[...] = jnp.zeros_like(q_norm_ref)
        k_norm_ref[...] = norm2(k_ref[...])

    q = heads_below(q_ref[...])
    q_norm_ref[...] = jnp.maximum(q_norm_ref[...], norm2(q))
    key = lax.broadcasted_iota(jnp.int32, (ROWS, COLS), 0)
    token = lax.broadcasted_iota(jnp.int32, (ROWS, COLS), 1) % ROWS
    for chunk in range(BLK // ROWS):
        @pl.when(step == chunk)
        def _():
            full = chunk * ROWS
            scores = dot_t(k_ref[full:full + ROWS, :], q) * SCALE
            weights = jnp.where(key <= token, jnp.exp2(scores), 0.0).astype(BF)
            if full:
                before = jnp.exp2(dot_t(k_ref[:full, :], q) * SCALE).astype(BF)
                weights = jnp.concatenate([before, weights], axis=0)
            state_ref[0] = dot(vt_ref[:, :full + ROWS], weights)


def own(queries, key_rows, value_rows):
    return pl.pallas_call(
        own_kernel,
        grid=(BLK // ROWS,),
        out_shape=(state_shape(), NORM, NORM),
        in_specs=[pl.BlockSpec((ROWS, GROUP * HD), lambda i: (i, 0)), same((BLK, HD)), same((BLK, HD))],
        out_specs=(STATE, same((8, HD)), same((8, HD))),
        scratch_shapes=[pltpu.VMEM((VROWS, BLK), BF)],
        compiler_params=params(),
        cost_estimate=pl.CostEstimate(flops=2 * 2 * 4096 * 512 * 128, bytes_accessed=4 << 20, transcendentals=4096 * 512),
        name="own",
    )(queries, key_rows, value_rows)


def lay(tags, payload_refs, anchors, k_ref, vt_ref):
    blocks = len(DZ)
    own_rows = blocks * KEEP
    parts = [ref[:own_rows, :] for ref in payload_refs]
    flags = [origin_visible(dx, dcore, b) for dx, dcore in tags for b in range(blocks)]
    if anchors:
        parts += [ref[own_rows:, :] for ref in anchors]
        flags += [lax.axis_index("ctx") >= 1] * len(anchors)
    rows = jnp.concatenate(parts, axis=0)
    k_ref[...] = rows[:, :HD]
    lane = lax.broadcasted_iota(jnp.int32, (1, 2 * KEEP), 1)
    row = lax.broadcasted_iota(jnp.int32, (16, 2 * KEEP), 0)
    for i in range(len(flags) // 2):
        cols = slice(i * 2 * KEEP, (i + 1) * 2 * KEEP)
        one = jnp.where(lane < KEEP, flags[2 * i].astype(F32), flags[2 * i + 1].astype(F32))
        vt_ref[:HD, cols] = (rows[cols, HD:].astype(F32).T * one).astype(BF)
        vt_ref[HD:, cols] = jnp.where(row == 0, one, 0.0).astype(BF)


def batch_kernel(tags, q_ref, state_in, *refs):
    n = len(tags)
    payloads, state_ref, norm_ref, k_ref, vt_ref = refs[:n], refs[n], refs[n + 1], refs[n + 2], refs[n + 3]

    @pl.when(pl.program_id(0) == 0)
    def _():
        lay(tags, payloads, (), k_ref, vt_ref)
        norm_ref[...] = norm2(k_ref[...])

    weights = jnp.exp2(dot_t(k_ref[...], heads_below(q_ref[...])) * SCALE).astype(BF)
    state_ref[0] = state_in[0] + dot(vt_ref[...], weights)


def batch(tags, queries, state, payloads, name):
    keys = len(tags) * len(DZ) * KEEP
    return pl.pallas_call(
        functools.partial(batch_kernel, tags),
        grid=(BLK // ROWS,),
        out_shape=(state_shape(), NORM),
        in_specs=[pl.BlockSpec((ROWS, GROUP * HD), lambda i: (i, 0)), STATE] + [same((PAY, 2 * HD))] * len(tags),
        out_specs=(STATE, same((8, HD))),
        scratch_shapes=[pltpu.VMEM((keys, HD), BF), pltpu.VMEM((VROWS, keys), BF)],
        compiler_params=params(),
        input_output_aliases={1: 0},
        cost_estimate=pl.CostEstimate(flops=2 * 2 * 4096 * keys * 128 * 2, bytes_accessed=6 << 20, transcendentals=4096 * keys),
        name=name,
    )(queries, state, *payloads)


def lay_kernel(tags, *refs):
    n, m = len(tags), len(tags) + X * CORES
    q_norm, norms = refs[m], refs[m + 1:m + 3]
    k_ref, vt_ref, plain_ref = refs[m + 3:]
    lay(tags, refs[:n], refs[n:m], k_ref, vt_ref)
    key_norm = jnp.maximum(jnp.maximum(norms[0][...], norms[1][...]), norm2(k_ref[...]))
    plain_ref[...] = (q_norm[...] * key_norm <= LIMIT).astype(F32)


def lay_out(tags, payloads, everything, norms):
    keys = (len(tags) * len(DZ) + X * CORES) * KEEP
    return pl.pallas_call(
        functools.partial(lay_kernel, tags),
        out_shape=(jax.ShapeDtypeStruct((keys, HD), BF), jax.ShapeDtypeStruct((VROWS, keys), BF), NORM),
        in_specs=[VMEM] * (len(tags) + X * CORES + 3),
        out_specs=(VMEM, VMEM, VMEM),
        compiler_params=params(),
        name="lay",
    )(*payloads, *everything, *norms)


def general(q_ref, k_own, v_own, payloads, chunk, heads, out_ref, stage, kv_own, peak_ref, total_ref, acc_ref, sem):
    q = heads_below(q_ref[...])
    width = q.shape[0]
    copies = [pltpu.make_async_copy(k_own, kv_own.at[0], sem.at[0]), pltpu.make_async_copy(v_own, kv_own.at[1], sem.at[1])]
    copies += [pltpu.make_async_copy(ref, stage.at[i], sem.at[2 + i]) for i, ref in enumerate(payloads)]
    for copy in copies:
        copy.start()
    for copy in copies:
        copy.wait()
    peak_ref[...] = jnp.full(peak_ref.shape, -1e30, F32)
    total_ref[...] = jnp.zeros(total_ref.shape, F32)
    acc_ref[...] = jnp.zeros(acc_ref.shape, F32)

    def take(keys, values, seen):
        scores = jnp.where(seen, dot_t(keys, q), -1e30)
        peak = peak_ref[0:1, :]
        new_peak = jnp.maximum(peak, jnp.max(scores, axis=0, keepdims=True))
        shrink = jnp.exp2((peak - new_peak) * SCALE)
        weights = jnp.where(seen, jnp.exp2((scores - new_peak) * SCALE), 0.0)
        peak_ref[0:1, :] = new_peak
        total_ref[0:1, :] = total_ref[0:1, :] * shrink + jnp.sum(weights, axis=0, keepdims=True)
        update = dot(values.astype(F32).T.astype(BF), weights.astype(BF))
        acc_ref[...] = acc_ref[...] * shrink + update

    token = chunk * ROWS + lax.broadcasted_iota(jnp.int32, (BLK, width), 1) % ROWS
    take(kv_own[0], kv_own[1], lax.broadcasted_iota(jnp.int32, (BLK, width), 0) <= token)
    me, z, x, core = place()
    row = lax.broadcasted_iota(jnp.int32, (PAY, width), 0) // KEEP

    def one(i, carry):
        base = ((x - i // CORES + X) % X) * CORES + (core + i % CORES) % CORES
        hosts = jnp.full((PAY, width), -1, jnp.int32)
        for b in range(len(DZ)):
            hosts = jnp.where(row == b, ((z - DZ[b] + Z) % Z) * (X * CORES) + base, hosts)
        rows = stage[i]
        take(rows[:, :HD], rows[:, HD:], hosts < me)
        return carry

    lax.fori_loop(0, jnp.where(me >= 1, X * CORES, 0), one, 0)
    result = acc_ref[...] / total_ref[0:1, :]
    for h in range(heads):
        out_ref[:, h * HD:(h + 1) * HD] = result[:, h * ROWS:(h + 1) * ROWS].T.astype(BF)


def final_kernel(off, heads, q_ref, state_in, k_ref, vt_ref, plain_ref, k_own, v_own, *refs):
    everything = refs[:X * CORES]
    out_ref, stage, kv_own, peak_ref, total_ref, acc_ref, sem = refs[X * CORES:]
    plain = plain_ref[0, 0] > 0.0
    chunk = chunk_of(off)
    q_ref = q_ref.at[pl.ds(pl.multiple_of(chunk * ROWS, ROWS), ROWS), :]

    @pl.when(plain)
    def _():
        for first in range(0, GROUP, heads):
            q = heads_below(q_ref[:, first * HD:(first + heads) * HD])
            weights = jnp.exp2(dot_t(k_ref[...], q) * SCALE).astype(BF)
            total = state_in[chunk, :, first * ROWS:(first + heads) * ROWS] + dot(vt_ref[...], weights)
            result = total[:HD] / total[HD:HD + 1]
            for h in range(heads):
                out_ref[:, (first + h) * HD:(first + h + 1) * HD] = result[:, h * ROWS:(h + 1) * ROWS].T.astype(BF)

    @pl.when(jnp.logical_not(plain))
    def _():
        general(q_ref, k_own, v_own, everything, chunk, GROUP, out_ref, stage, kv_own, peak_ref, total_ref, acc_ref, sem)


def chunk_of(off):
    return (lax.axis_index("tp") + off) % (BLK // ROWS)


def final(off, queries, state, keys, values, plain, key_rows, value_rows, everything, heads=FINAL_HEADS):
    count = keys.shape[0]
    width = COLS
    return pl.pallas_call(
        functools.partial(final_kernel, off, heads),
        in_specs=[
            VMEM, VMEM, VMEM, VMEM, VMEM,
        ] + [ANY] * (2 + X * CORES),
        out_specs=VMEM,
        scratch_shapes=[
            pltpu.VMEM((X * CORES, PAY, 2 * HD), BF), pltpu.VMEM((2, BLK, HD), BF),
            pltpu.VMEM((8, width), F32), pltpu.VMEM((8, width), F32), pltpu.VMEM((HD, width), F32),
            pltpu.SemaphoreType.DMA((2 + X * CORES,)),
        ],
        out_shape=jax.ShapeDtypeStruct((ROWS, GROUP * HD), BF),
        compiler_params=params(),
        cost_estimate=pl.CostEstimate(flops=2 * 2 * 1024 * count * 128 * 2, bytes_accessed=2 << 20, transcendentals=1024 * count),
        name="final",
    )(queries, state, keys, values, plain, key_rows, value_rows, *everything)


def host_of(z, x, core):
    return ((z % Z) * X + x % X) * CORES + core % CORES


ALL = [(z, x, c) for z in range(Z) for x in range(X) for c in range(CORES)]


def move(value, dz=0, dx=0, dcore=0):
    pairs = [(host_of(z, x, c), host_of(z + dz, x + dx, c + dcore)) for z, x, c in ALL]
    return lax.ppermute(value, "ctx", pairs)


def body(queries, key_rows, value_rows, keep_rows):
    me, z, x, core = place()
    passing, *pieces = select(keep_rows, key_rows, value_rows)

    pair = [pieces[0]] + [move(pieces[dx], dx=dx) for dx in (1, 2, 3)]
    state, q_norm, k_norm = own(queries, key_rows, value_rows)
    *pair, state = lax.optimization_barrier((*pair, state))
    pair = functools.reduce(lambda a, dx: jnp.where(x == dx, pair[dx], a), (1, 2, 3), pair[0])
    piece = jnp.where(core == 0, pair[:KEEP], move(pair[KEEP:], dcore=1))

    up, down = [jnp.concatenate([passing, piece], axis=0)], [None]
    down[0] = up[0]
    for step in range(4):
        up.append(move(up[-1], dz=1))
        if step < 3:
            down.append(move(down[-1], dz=-1))
    anchor = piece
    for step in (1, 2, 3, 4):
        anchor = jnp.where(z == step, up[step][KEEP:], anchor)
        if step < 4:
            anchor = jnp.where(z == Z - step, down[step][KEEP:], anchor)
    ring = (up[0], up[1], down[1], up[2], down[2], up[3], down[3], up[4])
    payload = jnp.concatenate([r[:KEEP] for r in ring] + [anchor], axis=0)

    across = {0: payload}
    for dx in (1, 3, 2):
        across[dx] = move(payload, dx=dx)
    other = {dx: move(across[dx], dcore=1) for dx in (0, 1, 3, 2)}
    everything = [v[dx] for dx in range(X) for v in (across, other)]

    state, near_norm = batch([(0, 0), (0, 1)], queries, state, [across[0], other[0]], "near")
    tags = [(dx, dc) for dx in (1, 3, 2) for dc in (0, 1)]
    payloads = [v[dx] for dx in (1, 3, 2) for v in (across, other)]
    keys, values, plain = lay_out(tags, payloads, everything, [q_norm, k_norm, near_norm])

    y = lax.axis_index("tp")
    ranks = lax.axis_size("tp")
    result = jnp.zeros((ROWS, ranks * GROUP * HD), BF)
    for off in (2, 1, 3, 0):
        part = final(off, queries, state, keys, values, plain, key_rows, value_rows, everything)
        if off:
            part = lax.ppermute(part, "tp", [(i, (i + off) % ranks) for i in range(ranks)])
        result = lax.dynamic_update_slice(result, part, (0, ((y - off) % ranks) * GROUP * HD))
    return result


def solution(mesh):
    in_specs = (P("ctx", "tp"), P("ctx", "tp"), P("ctx", "tp"), P("ctx", None))
    out_specs = P(("ctx", "tp"), None)
    return jax.shard_map(body, mesh=mesh, in_specs=in_specs, out_specs=out_specs, check_vma=False)
```

```python
import functools

import jax
import jax.numpy as jnp
from jax import lax
from jax.experimental import pallas as pl
from jax.experimental.pallas import tpu as pltpu
from jax.sharding import PartitionSpec as P

BF = jnp.bfloat16
F32 = jnp.float32
Z, X, CORES = 8, 4, 2
HD, GROUP, KEEP, BLK = 128, 8, 64, 512
VROWS = HD + 16
DZ = (0, 1, -1, 2, -2, 3, -3, 4)
PAY = (len(DZ) + 1) * KEEP
LOG2E = 1.4426950408889634
SCALE = HD ** (-0.5) * LOG2E
LIMIT = 75.0 * 75.0 * HD
ROWS = 128
COLS = ROWS * GROUP
FINAL_HEADS = 8
VMEM = pl.BlockSpec(memory_space=pltpu.VMEM)
ANY = pl.BlockSpec(memory_space=pl.ANY)
NORM = jax.ShapeDtypeStruct((8, HD), F32)


def params(mib=36):
    return pltpu.CompilerParams(vmem_limit_bytes=mib << 20)


def dot_t(a, b):
    return lax.dot_general(a, b, (((1,), (1,)), ((), ())), preferred_element_type=F32)


def dot(a, b):
    return lax.dot_general(a, b, (((1,), (0,)), ((), ())), preferred_element_type=F32)


def norm2(rows):
    rows = rows.astype(F32)
    most = jnp.max(jnp.sum(rows * rows, axis=1, keepdims=True), axis=0, keepdims=True)
    return jnp.broadcast_to(most, (8, HD))


def place():
    me = lax.axis_index("ctx")
    return me, me // (X * CORES), (me // CORES) % X, me % CORES


def origin_visible(dx, dcore, block):
    me, z, x, core = place()
    if block == len(DZ):
        return me >= 1
    host = ((z - DZ[block] + Z) % Z) * (X * CORES) + ((x - dx + X) % X) * CORES + (core + dcore) % CORES
    return host < me


def select_kernel(keep_ref, k_ref, v_ref, pass_ref, *piece_refs):
    chosen = (lax.broadcasted_iota(jnp.int32, (BLK, KEEP), 0) == keep_ref[...]).astype(BF)
    for side, ref in ((0, k_ref), (1, v_ref)):
        lanes = slice(side * HD, (side + 1) * HD)
        pass_ref[:, lanes] = lax.dot_general(
            chosen, ref[...], (((0,), (0,)), ((), ())), preferred_element_type=F32
        ).astype(BF)
        for x, piece_ref in enumerate(piece_refs):
            piece_ref[:, lanes] = ref[x * 2 * KEEP:(x + 1) * 2 * KEEP, :]


def same(shape):
    return pl.BlockSpec(shape, lambda *i: (0,) * len(shape))


def select(keep_rows, key_rows, value_rows):
    rows = [KEEP] + [2 * KEEP] * X
    return pl.pallas_call(
        select_kernel,
        grid=(1,),
        out_shape=tuple(jax.ShapeDtypeStruct((n, 2 * HD), BF) for n in rows),
        in_specs=[same((1, KEEP)), same((BLK, HD)), same((BLK, HD))],
        out_specs=tuple(same((n, 2 * HD)) for n in rows),
        compiler_params=params(60),
        name="select",
    )(keep_rows, key_rows, value_rows)


def heads_below(q):
    return jnp.concatenate([q[:, h * HD:(h + 1) * HD] for h in range(q.shape[1] // HD)], axis=0)


def state_shape():
    return jax.ShapeDtypeStruct((BLK // ROWS, VROWS, COLS), F32)


STATE = pl.BlockSpec((1, VROWS, COLS), lambda i: (i, 0, 0))


def lay(tags, payload_refs, anchors, k_ref, vt_ref):
    blocks = len(DZ)
    own_rows = blocks * KEEP
    parts = [ref[:own_rows, :] for ref in payload_refs]
    flags = [origin_visible(dx, dcore, b) for dx, dcore in tags for b in range(blocks)]
    if anchors:
        parts += [ref[own_rows:, :] for ref in anchors]
        flags += [lax.axis_index("ctx") >= 1] * len(anchors)
    rows = jnp.concatenate(parts, axis=0)
    k_ref[...] = rows[:, :HD]
    lane = lax.broadcasted_iota(jnp.int32, (1, 2 * KEEP), 1)
    row = lax.broadcasted_iota(jnp.int32, (16, 2 * KEEP), 0)
    for i in range(len(flags) // 2):
        cols = slice(i * 2 * KEEP, (i + 1) * 2 * KEEP)
        one = jnp.where(lane < KEEP, flags[2 * i].astype(F32), flags[2 * i + 1].astype(F32))
        vt_ref[:HD, cols] = (rows[cols, HD:].astype(F32).T * one).astype(BF)
        vt_ref[HD:, cols] = jnp.where(row == 0, one, 0.0).astype(BF)


def early_kernel(tags, q_ref, k_own, v_own, *refs):
    n = len(tags)
    payloads = refs[:n]
    state_ref, q_norm_ref, k_norm_ref, k_ref, vt_ref = refs[n:]
    step = pl.program_id(0)
    near = k_ref.shape[0]

    @pl.when(step == 0)
    def _():
        lay(tags, payloads, (), k_ref, vt_ref)
        vt_ref[:HD, near:] = v_own[...].astype(F32).T.astype(BF)
        rows = lax.broadcasted_iota(jnp.int32, (16, BLK), 0)
        vt_ref[HD:, near:] = jnp.where(rows == 0, 1.0, 0.0).astype(BF)
        q_norm_ref[...] = jnp.zeros_like(q_norm_ref)
        k_norm_ref[...] = jnp.maximum(norm2(k_own[...]), norm2(k_ref[...]))

    q = heads_below(q_ref[...])
    q_norm_ref[...] = jnp.maximum(q_norm_ref[...], norm2(q))
    key = lax.broadcasted_iota(jnp.int32, (ROWS, COLS), 0)
    token = lax.broadcasted_iota(jnp.int32, (ROWS, COLS), 1) % ROWS
    for chunk in range(BLK // ROWS):
        @pl.when(step == chunk)
        def _():
            full = chunk * ROWS
            weights = [jnp.exp2(dot_t(k_ref[...], q) * SCALE).astype(BF)]
            if full:
                weights.append(jnp.exp2(dot_t(k_own[:full, :], q) * SCALE).astype(BF))
            scores = dot_t(k_own[full:full + ROWS, :], q) * SCALE
            weights.append(jnp.where(key <= token, jnp.exp2(scores), 0.0).astype(BF))
            state_ref[0] = dot(vt_ref[:, :near + full + ROWS], jnp.concatenate(weights, axis=0))


def early(tags, queries, key_rows, value_rows, payloads):
    near = len(tags) * len(DZ) * KEEP
    cost = 4096 * (near + BLK) * HD
    return pl.pallas_call(
        functools.partial(early_kernel, tags),
        grid=(BLK // ROWS,),
        out_shape=(state_shape(), NORM, NORM),
        in_specs=[
            pl.BlockSpec((ROWS, GROUP * HD), lambda i: (i, 0)), same((BLK, HD)), same((BLK, HD)),
        ] + [same((PAY, 2 * HD))] * len(tags),
        out_specs=(STATE, same((8, HD)), same((8, HD))),
        scratch_shapes=[pltpu.VMEM((near, HD), BF), pltpu.VMEM((VROWS, near + BLK), BF)],
        compiler_params=params(),
        cost_estimate=pl.CostEstimate(flops=8 * cost, bytes_accessed=4 << 20, transcendentals=cost // HD),
        name="early",
    )(queries, key_rows, value_rows, *payloads)


def lay_kernel(tags, *refs):
    n, m = len(tags), len(tags) + X * CORES
    q_norm, norms = refs[m], refs[m + 1]
    k_ref, vt_ref, plain_ref = refs[m + 2:]
    lay(tags, refs[:n], refs[n:m], k_ref, vt_ref)
    key_norm = jnp.maximum(norms[...], norm2(k_ref[...]))
    plain_ref[...] = (q_norm[...] * key_norm <= LIMIT).astype(F32)


def lay_out(tags, payloads, everything, norms):
    keys = (len(tags) * len(DZ) + X * CORES) * KEEP
    return pl.pallas_call(
        functools.partial(lay_kernel, tags),
        out_shape=(jax.ShapeDtypeStruct((keys, HD), BF), jax.ShapeDtypeStruct((VROWS, keys), BF), NORM),
        in_specs=[VMEM] * (len(tags) + X * CORES + 2),
        out_specs=(VMEM, VMEM, VMEM),
        compiler_params=params(),
        name="lay",
    )(*payloads, *everything, *norms)


def general(q_ref, k_own, v_own, payloads, chunk, heads, out_ref, stage, kv_own, peak_ref, total_ref, acc_ref, sem):
    q = heads_below(q_ref[...])
    width = q.shape[0]
    copies = [pltpu.make_async_copy(k_own, kv_own.at[0], sem.at[0]), pltpu.make_async_copy(v_own, kv_own.at[1], sem.at[1])]
    copies += [pltpu.make_async_copy(ref, stage.at[i], sem.at[2 + i]) for i, ref in enumerate(payloads)]
    for copy in copies:
        copy.start()
    for copy in copies:
        copy.wait()
    peak_ref[...] = jnp.full(peak_ref.shape, -1e30, F32)
    total_ref[...] = jnp.zeros(total_ref.shape, F32)
    acc_ref[...] = jnp.zeros(acc_ref.shape, F32)

    def take(keys, values, seen):
        scores = jnp.where(seen, dot_t(keys, q), -1e30)
        peak = peak_ref[0:1, :]
        new_peak = jnp.maximum(peak, jnp.max(scores, axis=0, keepdims=True))
        shrink = jnp.exp2((peak - new_peak) * SCALE)
        weights = jnp.where(seen, jnp.exp2((scores - new_peak) * SCALE), 0.0)
        peak_ref[0:1, :] = new_peak
        total_ref[0:1, :] = total_ref[0:1, :] * shrink + jnp.sum(weights, axis=0, keepdims=True)
        update = dot(values.astype(F32).T.astype(BF), weights.astype(BF))
        acc_ref[...] = acc_ref[...] * shrink + update

    token = chunk * ROWS + lax.broadcasted_iota(jnp.int32, (BLK, width), 1) % ROWS
    take(kv_own[0], kv_own[1], lax.broadcasted_iota(jnp.int32, (BLK, width), 0) <= token)
    me, z, x, core = place()
    row = lax.broadcasted_iota(jnp.int32, (PAY, width), 0) // KEEP

    def one(i, carry):
        base = ((x - i // CORES + X) % X) * CORES + (core + i % CORES) % CORES
        hosts = jnp.full((PAY, width), -1, jnp.int32)
        for b in range(len(DZ)):
            hosts = jnp.where(row == b, ((z - DZ[b] + Z) % Z) * (X * CORES) + base, hosts)
        rows = stage[i]
        take(rows[:, :HD], rows[:, HD:], hosts < me)
        return carry

    lax.fori_loop(0, jnp.where(me >= 1, X * CORES, 0), one, 0)
    result = acc_ref[...] / total_ref[0:1, :]
    for h in range(heads):
        out_ref[:, h * HD:(h + 1) * HD] = result[:, h * ROWS:(h + 1) * ROWS].T.astype(BF)


def final_kernel(off, heads, q_ref, state_in, k_ref, vt_ref, plain_ref, k_own, v_own, *refs):
    everything = refs[:X * CORES]
    out_ref, stage, kv_own, peak_ref, total_ref, acc_ref, sem = refs[X * CORES:]
    plain = plain_ref[0, 0] > 0.0
    chunk = chunk_of(off)
    q_ref = q_ref.at[pl.ds(pl.multiple_of(chunk * ROWS, ROWS), ROWS), :]

    @pl.when(plain)
    def _():
        for first in range(0, GROUP, heads):
            q = heads_below(q_ref[:, first * HD:(first + heads) * HD])
            weights = jnp.exp2(dot_t(k_ref[...], q) * SCALE).astype(BF)
            total = state_in[chunk, :, first * ROWS:(first + heads) * ROWS] + dot(vt_ref[...], weights)
            result = total[:HD] / total[HD:HD + 1]
            for h in range(heads):
                out_ref[:, (first + h) * HD:(first + h + 1) * HD] = result[:, h * ROWS:(h + 1) * ROWS].T.astype(BF)

    @pl.when(jnp.logical_not(plain))
    def _():
        general(q_ref, k_own, v_own, everything, chunk, GROUP, out_ref, stage, kv_own, peak_ref, total_ref, acc_ref, sem)


def chunk_of(off):
    return (lax.axis_index("tp") + off) % (BLK // ROWS)


def final(off, queries, state, keys, values, plain, key_rows, value_rows, everything, heads=FINAL_HEADS):
    count = keys.shape[0]
    width = COLS
    return pl.pallas_call(
        functools.partial(final_kernel, off, heads),
        in_specs=[
            VMEM, VMEM, VMEM, VMEM, VMEM,
        ] + [ANY] * (2 + X * CORES),
        out_specs=VMEM,
        scratch_shapes=[
            pltpu.VMEM((X * CORES, PAY, 2 * HD), BF), pltpu.VMEM((2, BLK, HD), BF),
            pltpu.VMEM((8, width), F32), pltpu.VMEM((8, width), F32), pltpu.VMEM((HD, width), F32),
            pltpu.SemaphoreType.DMA((2 + X * CORES,)),
        ],
        out_shape=jax.ShapeDtypeStruct((ROWS, GROUP * HD), BF),
        compiler_params=params(),
        cost_estimate=pl.CostEstimate(flops=2 * 2 * 1024 * count * 128 * 2, bytes_accessed=2 << 20, transcendentals=1024 * count),
        name="final",
    )(queries, state, keys, values, plain, key_rows, value_rows, *everything)


def join_kernel(order, *refs):
    parts, out_ref, sem = refs[:-2], refs[-2], refs[-1]
    y = lax.axis_index("tp")
    width = GROUP * HD
    copies = []
    for i, part in enumerate(parts):
        first = pl.multiple_of((y - order[i] + len(parts)) % len(parts) * width, width)
        copies.append(pltpu.make_async_copy(part, out_ref.at[:, pl.ds(first, width)], sem.at[i]))
    for copy in copies:
        copy.start()
    for copy in copies:
        copy.wait()


def join(order, parts):
    return pl.pallas_call(
        functools.partial(join_kernel, order),
        out_shape=jax.ShapeDtypeStruct((ROWS, len(parts) * GROUP * HD), BF),
        in_specs=[ANY] * len(parts),
        out_specs=ANY,
        scratch_shapes=[pltpu.SemaphoreType.DMA((len(parts),))],
        compiler_params=params(),
        name="join",
    )(*parts)


def host_of(z, x, core):
    return ((z % Z) * X + x % X) * CORES + core % CORES


ALL = [(z, x, c) for z in range(Z) for x in range(X) for c in range(CORES)]


def move(value, dz=0, dx=0, dcore=0):
    pairs = [(host_of(z, x, c), host_of(z + dz, x + dx, c + dcore)) for z, x, c in ALL]
    return lax.ppermute(value, "ctx", pairs)


def body(queries, key_rows, value_rows, keep_rows):
    me, z, x, core = place()
    passing, *pieces = select(keep_rows, key_rows, value_rows)

    pair = [pieces[0]] + [move(pieces[dx], dx=dx) for dx in (1, 2, 3)]
    pair = functools.reduce(lambda a, dx: jnp.where(x == dx, pair[dx], a), (1, 2, 3), pair[0])
    piece = jnp.where(core == 0, pair[:KEEP], move(pair[KEEP:], dcore=1))

    up, down = [jnp.concatenate([passing, piece], axis=0)], [None]
    down[0] = up[0]
    for step in range(4):
        up.append(move(up[-1], dz=1))
        if step < 3:
            down.append(move(down[-1], dz=-1))
    anchor = piece
    for step in (1, 2, 3, 4):
        anchor = jnp.where(z == step, up[step][KEEP:], anchor)
        if step < 4:
            anchor = jnp.where(z == Z - step, down[step][KEEP:], anchor)
    ring = (up[0], up[1], down[1], up[2], down[2], up[3], down[3], up[4])
    payload = jnp.concatenate([r[:KEEP] for r in ring] + [anchor], axis=0)

    across = {0: payload}
    for dx in (1, 3, 2):
        across[dx] = move(payload, dx=dx)
    other = {0: move(across[0], dcore=1)}
    state, q_norm, k_norm = early([(0, 0), (0, 1)], queries, key_rows, value_rows, [across[0], other[0]])
    across[1], across[3], across[2], state = lax.optimization_barrier((across[1], across[3], across[2], state))
    for dx in (1, 3, 2):
        other[dx] = move(across[dx], dcore=1)
    everything = [v[dx] for dx in range(X) for v in (across, other)]

    tags = [(dx, dc) for dx in (1, 3, 2) for dc in (0, 1)]
    payloads = [v[dx] for dx in (1, 3, 2) for v in (across, other)]
    keys, values, plain = lay_out(tags, payloads, everything, [q_norm, k_norm])

    ranks = lax.axis_size("tp")
    parts = {}
    order = (0, 2, 1, 3)
    for off in order:
        part = final(off, queries, state, keys, values, plain, key_rows, value_rows, everything)
        if off:
            part = lax.ppermute(part, "tp", [(i, (i + off) % ranks) for i in range(ranks)])
        parts[off] = part
    return join(order, [parts[off] for off in order])


def solution(mesh):
    in_specs = (P("ctx", "tp"), P("ctx", "tp"), P("ctx", "tp"), P("ctx", None))
    out_specs = P(("ctx", "tp"), None)
    return jax.shard_map(body, mesh=mesh, in_specs=in_specs, out_specs=out_specs, check_vma=False)
```

```python
import functools

import jax
import jax.numpy as jnp
from jax import lax
from jax.experimental import pallas as pl
from jax.experimental.pallas import tpu as pltpu
from jax.sharding import PartitionSpec as P

BF = jnp.bfloat16
F32 = jnp.float32
Z, X, CORES = 8, 4, 2
HD, GROUP, KEEP, BLK = 128, 8, 64, 512
VROWS = HD + 16
DZ = (0, 1, -1, 2, -2, 3, -3, 4)
PAY = (len(DZ) + 1) * KEEP
LOG2E = 1.4426950408889634
SCALE = HD ** (-0.5) * LOG2E
LIMIT = 75.0 * 75.0 * HD
ROWS = 128
COLS = ROWS * GROUP
VMEM = pl.BlockSpec(memory_space=pltpu.VMEM)
ANY = pl.BlockSpec(memory_space=pl.ANY)
NORM = jax.ShapeDtypeStruct((8, HD), F32)


def params(mib=36):
    return pltpu.CompilerParams(vmem_limit_bytes=mib << 20)


def dot_t(a, b):
    return lax.dot_general(a, b, (((1,), (1,)), ((), ())), preferred_element_type=F32)


def dot(a, b):
    return lax.dot_general(a, b, (((1,), (0,)), ((), ())), preferred_element_type=F32)


def norm2(rows):
    rows = rows.astype(F32)
    most = jnp.max(jnp.sum(rows * rows, axis=1, keepdims=True), axis=0, keepdims=True)
    return jnp.broadcast_to(most, (8, HD))


def place():
    me = lax.axis_index("ctx")
    return me, me // (X * CORES), (me // CORES) % X, me % CORES


def origin_visible(dx, dcore, block):
    me, z, x, core = place()
    if block == len(DZ):
        return me >= 1
    host = ((z - DZ[block] + Z) % Z) * (X * CORES) + ((x - dx + X) % X) * CORES + (core + dcore) % CORES
    return host < me


def select_kernel(keep_ref, k_ref, v_ref, pass_ref, *piece_refs):
    chosen = (lax.broadcasted_iota(jnp.int32, (BLK, KEEP), 0) == keep_ref[...]).astype(BF)
    for side, ref in ((0, k_ref), (1, v_ref)):
        lanes = slice(side * HD, (side + 1) * HD)
        pass_ref[:, lanes] = lax.dot_general(
            chosen, ref[...], (((0,), (0,)), ((), ())), preferred_element_type=F32
        ).astype(BF)
        for x, piece_ref in enumerate(piece_refs):
            piece_ref[:, lanes] = ref[x * 2 * KEEP:(x + 1) * 2 * KEEP, :]


def same(shape):
    return pl.BlockSpec(shape, lambda *i: (0,) * len(shape))


def select(keep_rows, key_rows, value_rows):
    rows = [KEEP] + [2 * KEEP] * X
    return pl.pallas_call(
        select_kernel,
        grid=(1,),
        out_shape=tuple(jax.ShapeDtypeStruct((n, 2 * HD), BF) for n in rows),
        in_specs=[same((1, KEEP)), same((BLK, HD)), same((BLK, HD))],
        out_specs=tuple(same((n, 2 * HD)) for n in rows),
        compiler_params=params(60),
        name="select",
    )(keep_rows, key_rows, value_rows)


def heads_below(q):
    return jnp.concatenate([q[:, h * HD:(h + 1) * HD] for h in range(q.shape[1] // HD)], axis=0)


def state_shape():
    return jax.ShapeDtypeStruct((BLK // ROWS, VROWS, COLS), F32)


STATE = pl.BlockSpec((1, VROWS, COLS), lambda i: (i, 0, 0))


def lay(tags, payload_refs, anchors, k_ref, vt_ref):
    blocks = len(DZ)
    own_rows = blocks * KEEP
    parts = [ref[:own_rows, :] for ref in payload_refs]
    flags = [origin_visible(dx, dcore, b) for dx, dcore in tags for b in range(blocks)]
    if anchors:
        parts += [ref[own_rows:, :] for ref in anchors]
        flags += [lax.axis_index("ctx") >= 1] * len(anchors)
    rows = jnp.concatenate(parts, axis=0)
    k_ref[...] = rows[:, :HD]
    lane = lax.broadcasted_iota(jnp.int32, (1, 2 * KEEP), 1)
    row = lax.broadcasted_iota(jnp.int32, (16, 2 * KEEP), 0)
    for i in range(len(flags) // 2):
        cols = slice(i * 2 * KEEP, (i + 1) * 2 * KEEP)
        one = jnp.where(lane < KEEP, flags[2 * i].astype(F32), flags[2 * i + 1].astype(F32))
        vt_ref[:HD, cols] = (rows[cols, HD:].astype(F32).T * one).astype(BF)
        vt_ref[HD:, cols] = jnp.where(row == 0, one, 0.0).astype(BF)


def early_kernel(tags, q_ref, k_own, v_own, *refs):
    n = len(tags)
    payloads = refs[:n]
    state_ref, q_norm_ref, k_norm_ref, k_ref, vt_ref = refs[n:]
    step = pl.program_id(0)
    near = k_ref.shape[0]

    @pl.when(step == 0)
    def _():
        lay(tags, payloads, (), k_ref, vt_ref)
        vt_ref[:HD, near:] = v_own[...].astype(F32).T.astype(BF)
        rows = lax.broadcasted_iota(jnp.int32, (16, BLK), 0)
        vt_ref[HD:, near:] = jnp.where(rows == 0, 1.0, 0.0).astype(BF)
        q_norm_ref[...] = jnp.zeros_like(q_norm_ref)
        k_norm_ref[...] = jnp.maximum(norm2(k_own[...]), norm2(k_ref[...]))

    q = heads_below(q_ref[...])
    q_norm_ref[...] = jnp.maximum(q_norm_ref[...], norm2(q))
    key = lax.broadcasted_iota(jnp.int32, (ROWS, COLS), 0)
    token = lax.broadcasted_iota(jnp.int32, (ROWS, COLS), 1) % ROWS
    for chunk in range(BLK // ROWS):
        @pl.when(step == chunk)
        def _():
            full = chunk * ROWS
            weights = [jnp.exp2(dot_t(k_ref[...], q) * SCALE).astype(BF)]
            if full:
                weights.append(jnp.exp2(dot_t(k_own[:full, :], q) * SCALE).astype(BF))
            scores = dot_t(k_own[full:full + ROWS, :], q) * SCALE
            weights.append(jnp.where(key <= token, jnp.exp2(scores), 0.0).astype(BF))
            state_ref[0] = dot(vt_ref[:, :near + full + ROWS], jnp.concatenate(weights, axis=0))


def early(tags, queries, key_rows, value_rows, payloads):
    near = len(tags) * len(DZ) * KEEP
    cost = 4096 * (near + BLK) * HD
    return pl.pallas_call(
        functools.partial(early_kernel, tags),
        grid=(BLK // ROWS,),
        out_shape=(state_shape(), NORM, NORM),
        in_specs=[
            pl.BlockSpec((ROWS, GROUP * HD), lambda i: (i, 0)), same((BLK, HD)), same((BLK, HD)),
        ] + [same((PAY, 2 * HD))] * len(tags),
        out_specs=(STATE, same((8, HD)), same((8, HD))),
        scratch_shapes=[pltpu.VMEM((near, HD), BF), pltpu.VMEM((VROWS, near + BLK), BF)],
        compiler_params=params(),
        cost_estimate=pl.CostEstimate(flops=8 * cost, bytes_accessed=4 << 20, transcendentals=cost // HD),
        name="early",
    )(queries, key_rows, value_rows, *payloads)


def general(queries, k_own, v_own, payloads, out, q_ref, out_ref, stage, kv_own, peak_ref, total_ref, acc_ref, sem):
    copies = [pltpu.make_async_copy(k_own, kv_own.at[0], sem.at[0]), pltpu.make_async_copy(v_own, kv_own.at[1], sem.at[1])]
    copies += [pltpu.make_async_copy(ref, stage.at[i], sem.at[2 + i]) for i, ref in enumerate(payloads)]
    for copy in copies:
        copy.start()
    for copy in copies:
        copy.wait()
    me, z, x, core = place()

    def one_chunk(chunk, carry):
        rows = pl.ds(pl.multiple_of(chunk * ROWS, ROWS), ROWS)
        pltpu.sync_copy(queries.at[rows, :], q_ref)
        q = heads_below(q_ref[...])
        peak_ref[...] = jnp.full(peak_ref.shape, -1e30, F32)
        total_ref[...] = jnp.zeros(total_ref.shape, F32)
        acc_ref[...] = jnp.zeros(acc_ref.shape, F32)

        def take(keys, values, seen):
            scores = jnp.where(seen, dot_t(keys, q), -1e30)
            peak = peak_ref[0:1, :]
            new_peak = jnp.maximum(peak, jnp.max(scores, axis=0, keepdims=True))
            shrink = jnp.exp2((peak - new_peak) * SCALE)
            weights = jnp.where(seen, jnp.exp2((scores - new_peak) * SCALE), 0.0)
            peak_ref[0:1, :] = new_peak
            total_ref[0:1, :] = total_ref[0:1, :] * shrink + jnp.sum(weights, axis=0, keepdims=True)
            update = dot(values.astype(F32).T.astype(BF), weights.astype(BF))
            acc_ref[...] = acc_ref[...] * shrink + update

        token = chunk * ROWS + lax.broadcasted_iota(jnp.int32, (BLK, COLS), 1) % ROWS
        take(kv_own[0], kv_own[1], lax.broadcasted_iota(jnp.int32, (BLK, COLS), 0) <= token)
        row = lax.broadcasted_iota(jnp.int32, (PAY, COLS), 0) // KEEP

        def one(i, inner):
            base = ((x - i // CORES + X) % X) * CORES + (core + i % CORES) % CORES
            hosts = jnp.full((PAY, COLS), -1, jnp.int32)
            for b in range(len(DZ)):
                hosts = jnp.where(row == b, ((z - DZ[b] + Z) % Z) * (X * CORES) + base, hosts)
            rows = stage[i]
            take(rows[:, :HD], rows[:, HD:], hosts < me)
            return inner

        lax.fori_loop(0, jnp.where(me >= 1, X * CORES, 0), one, 0)
        result = acc_ref[...] / total_ref[0:1, :]
        for h in range(GROUP):
            out_ref[:, h * HD:(h + 1) * HD] = result[:, h * ROWS:(h + 1) * ROWS].T.astype(BF)
        pltpu.sync_copy(out_ref, out.at[rows, :])
        return carry

    lax.fori_loop(0, BLK // ROWS, one_chunk, 0)


def lay_kernel(tags, *refs):
    n, m = len(tags), len(tags) + X * CORES
    q_norm, norms, queries, k_own, v_own = refs[m:m + 5]
    k_ref, vt_ref, plain_ref, out, *scratch = refs[m + 5:]
    lay(tags, refs[:n], refs[n:m], k_ref, vt_ref)
    key_norm = jnp.maximum(norms[...], norm2(k_ref[...]))
    plain = (q_norm[...] * key_norm <= LIMIT).astype(F32)
    plain_ref[...] = plain

    @pl.when(plain[0, 0] <= 0.0)
    def _():
        general(queries, k_own, v_own, refs[n:m], out, *scratch)


def lay_out(tags, payloads, everything, norms, queries, key_rows, value_rows):
    keys = (len(tags) * len(DZ) + X * CORES) * KEEP
    return pl.pallas_call(
        functools.partial(lay_kernel, tags),
        out_shape=(
            jax.ShapeDtypeStruct((keys, HD), BF), jax.ShapeDtypeStruct((VROWS, keys), BF), NORM,
            jax.ShapeDtypeStruct(queries.shape, BF),
        ),
        in_specs=[VMEM] * (len(tags) + X * CORES + 2) + [ANY] * 3,
        out_specs=(VMEM, VMEM, VMEM, ANY),
        scratch_shapes=[
            pltpu.VMEM((ROWS, GROUP * HD), BF), pltpu.VMEM((ROWS, GROUP * HD), BF),
            pltpu.VMEM((X * CORES, PAY, 2 * HD), BF), pltpu.VMEM((2, BLK, HD), BF),
            pltpu.VMEM((8, COLS), F32), pltpu.VMEM((8, COLS), F32), pltpu.VMEM((HD, COLS), F32),
            pltpu.SemaphoreType.DMA((2 + X * CORES,)),
        ],
        compiler_params=params(),
        name="lay",
    )(*payloads, *everything, *norms, queries, key_rows, value_rows)


def chunk_of(off):
    return (lax.axis_index("tp") + off) % (BLK // ROWS)


def final_kernel(off, q_ref, state_in, k_ref, vt_ref, plain_ref, general_out, *rest):
    out_ref = rest[-1]
    plain = plain_ref[0, 0] > 0.0
    chunk = chunk_of(off)
    rows = pl.ds(pl.multiple_of(chunk * ROWS, ROWS), ROWS)

    @pl.when(plain)
    def _():
        weights = jnp.exp2(dot_t(k_ref[...], heads_below(q_ref[rows, :])) * SCALE).astype(BF)
        total = state_in[chunk] + dot(vt_ref[...], weights)
        result = total[:HD] / total[HD:HD + 1]
        for h in range(GROUP):
            out_ref[:, h * HD:(h + 1) * HD] = result[:, h * ROWS:(h + 1) * ROWS].T.astype(BF)

    @pl.when(jnp.logical_not(plain))
    def _():
        pltpu.sync_copy(general_out.at[rows, :], out_ref)


def final(off, queries, state, keys, values, plain, general_out, others):
    count = keys.shape[0]
    return pl.pallas_call(
        functools.partial(final_kernel, off),
        in_specs=[VMEM, VMEM, VMEM, VMEM, VMEM, ANY] + [ANY] * len(others),
        out_specs=VMEM,
        out_shape=jax.ShapeDtypeStruct((ROWS, GROUP * HD), BF),
        compiler_params=params(),
        cost_estimate=pl.CostEstimate(flops=2 * 2 * 1024 * count * 128 * 2, bytes_accessed=2 << 20, transcendentals=1024 * count),
        name="final",
    )(queries, state, keys, values, plain, general_out, *others)


def join_kernel(order, *refs):
    parts, out_ref, sem = refs[:-2], refs[-2], refs[-1]
    y = lax.axis_index("tp")
    width = GROUP * HD
    copies = []
    for i, part in enumerate(parts):
        first = pl.multiple_of((y - order[i] + len(parts)) % len(parts) * width, width)
        copies.append(pltpu.make_async_copy(part, out_ref.at[:, pl.ds(first, width)], sem.at[i]))
    for copy in copies:
        copy.start()
    for copy in copies:
        copy.wait()


def join(order, parts):
    return pl.pallas_call(
        functools.partial(join_kernel, order),
        out_shape=jax.ShapeDtypeStruct((ROWS, len(parts) * GROUP * HD), BF),
        in_specs=[ANY] * len(parts),
        out_specs=ANY,
        scratch_shapes=[pltpu.SemaphoreType.DMA((len(parts),))],
        compiler_params=params(),
        name="join",
    )(*parts)


def host_of(z, x, core):
    return ((z % Z) * X + x % X) * CORES + core % CORES


ALL = [(z, x, c) for z in range(Z) for x in range(X) for c in range(CORES)]


def move(value, dz=0, dx=0, dcore=0):
    pairs = [(host_of(z, x, c), host_of(z + dz, x + dx, c + dcore)) for z, x, c in ALL]
    return lax.ppermute(value, "ctx", pairs)


def body(queries, key_rows, value_rows, keep_rows):
    me, z, x, core = place()
    passing, *pieces = select(keep_rows, key_rows, value_rows)

    pair = [pieces[0]] + [move(pieces[dx], dx=dx) for dx in (1, 2, 3)]
    pair = functools.reduce(lambda a, dx: jnp.where(x == dx, pair[dx], a), (1, 2, 3), pair[0])
    piece = jnp.where(core == 0, pair[:KEEP], move(pair[KEEP:], dcore=1))

    here = jnp.concatenate([passing, piece], axis=0)
    planes = {0: here}
    for dz in (2, -2, 1, -1):
        planes[dz] = move(here, dz=dz)
    planes[4] = move(planes[-2], dz=-2)
    planes[3] = move(planes[2], dz=1)
    planes[-3] = move(planes[-2], dz=-1)
    anchor = piece
    for dz, plane in planes.items():
        if dz:
            anchor = jnp.where(z == dz % Z, plane[KEEP:], anchor)
    payload = jnp.concatenate([planes[dz][:KEEP] for dz in DZ] + [anchor], axis=0)

    across = {0: payload}
    for dx in (1, 3, 2):
        across[dx] = move(payload, dx=dx)
    other = {0: move(across[0], dcore=1)}
    state, q_norm, k_norm = early([(0, 0), (0, 1)], queries, key_rows, value_rows, [across[0], other[0]])
    across[1], across[3], across[2], state = lax.optimization_barrier((across[1], across[3], across[2], state))
    for dx in (1, 3, 2):
        other[dx] = move(across[dx], dcore=1)
    everything = [v[dx] for dx in range(X) for v in (across, other)]

    tags = [(dx, dc) for dx in (1, 3, 2) for dc in (0, 1)]
    payloads = [v[dx] for dx in (1, 3, 2) for v in (across, other)]
    keys, values, plain, general_out = lay_out(
        tags, payloads, everything, [q_norm, k_norm], queries, key_rows, value_rows)

    ranks = lax.axis_size("tp")
    parts = {}
    order = (0, 3, 1, 2)
    for off in order:
        part = final(off, queries, state, keys, values, plain, general_out, everything)
        if off:
            part = lax.ppermute(part, "tp", [(i, (i + off) % ranks) for i in range(ranks)])
        parts[off] = part
    return join(order, [parts[off] for off in order])


def solution(mesh):
    in_specs = (P("ctx", "tp"), P("ctx", "tp"), P("ctx", "tp"), P("ctx", None))
    out_specs = P(("ctx", "tp"), None)
    return jax.shard_map(body, mesh=mesh, in_specs=in_specs, out_specs=out_specs, check_vma=False)
```

```python
import functools

import jax
import jax.numpy as jnp
from jax import lax
from jax.experimental import pallas as pl
from jax.experimental.pallas import tpu as pltpu
from jax.sharding import PartitionSpec as P

BF = jnp.bfloat16
F32 = jnp.float32
Z, X, CORES = 8, 4, 2
HD, GROUP, KEEP, BLK = 128, 8, 64, 512
VROWS = HD + 16
DZ = (0, 1, -1, 2, -2, 3, -3, 4)
PAY = (len(DZ) + 1) * KEEP
LOG2E = 1.4426950408889634
SCALE = HD ** (-0.5) * LOG2E
LIMIT = 75.0 * 75.0 * HD
ROWS = 128
COLS = ROWS * GROUP
VMEM = pl.BlockSpec(memory_space=pltpu.VMEM)
ANY = pl.BlockSpec(memory_space=pl.ANY)
NORM = jax.ShapeDtypeStruct((8, HD), F32)


def params(mib=36):
    return pltpu.CompilerParams(vmem_limit_bytes=mib << 20)


def dot_t(a, b):
    return lax.dot_general(a, b, (((1,), (1,)), ((), ())), preferred_element_type=F32)


def dot(a, b):
    return lax.dot_general(a, b, (((1,), (0,)), ((), ())), preferred_element_type=F32)


def norm2(rows):
    rows = rows.astype(F32)
    most = jnp.max(jnp.sum(rows * rows, axis=1, keepdims=True), axis=0, keepdims=True)
    return jnp.broadcast_to(most, (8, HD))


def place():
    me = lax.axis_index("ctx")
    return me, me // (X * CORES), (me // CORES) % X, me % CORES


def origin_visible(dx, dcore, block):
    me, z, x, core = place()
    if block == len(DZ):
        return me >= 1
    host = ((z - DZ[block] + Z) % Z) * (X * CORES) + ((x - dx + X) % X) * CORES + (core + dcore) % CORES
    return host < me


def select_kernel(keep_ref, k_ref, v_ref, pass_ref, *piece_refs):
    chosen = (lax.broadcasted_iota(jnp.int32, (BLK, KEEP), 0) == keep_ref[...]).astype(BF)
    for side, ref in ((0, k_ref), (1, v_ref)):
        lanes = slice(side * HD, (side + 1) * HD)
        pass_ref[:, lanes] = lax.dot_general(
            chosen, ref[...], (((0,), (0,)), ((), ())), preferred_element_type=F32
        ).astype(BF)
        for x, piece_ref in enumerate(piece_refs):
            piece_ref[:, lanes] = ref[x * 2 * KEEP:(x + 1) * 2 * KEEP, :]


def same(shape):
    return pl.BlockSpec(shape, lambda *i: (0,) * len(shape))


def select(keep_rows, key_rows, value_rows):
    rows = [KEEP] + [2 * KEEP] * X
    return pl.pallas_call(
        select_kernel,
        grid=(1,),
        out_shape=tuple(jax.ShapeDtypeStruct((n, 2 * HD), BF) for n in rows),
        in_specs=[same((1, KEEP)), same((BLK, HD)), same((BLK, HD))],
        out_specs=tuple(same((n, 2 * HD)) for n in rows),
        compiler_params=params(60),
        name="select",
    )(keep_rows, key_rows, value_rows)


def heads_below(q):
    return jnp.concatenate([q[:, h * HD:(h + 1) * HD] for h in range(q.shape[1] // HD)], axis=0)


def state_shape():
    return jax.ShapeDtypeStruct((BLK // ROWS, VROWS, COLS), F32)


STATE = pl.BlockSpec((1, VROWS, COLS), lambda i: (i, 0, 0))


def lay(tags, payload_refs, anchors, k_ref, vt_ref):
    blocks = len(DZ)
    own_rows = blocks * KEEP
    parts = [ref[:own_rows, :] for ref in payload_refs]
    flags = [origin_visible(dx, dcore, b) for dx, dcore in tags for b in range(blocks)]
    if anchors:
        parts += [ref[own_rows:, :] for ref in anchors]
        flags += [lax.axis_index("ctx") >= 1] * len(anchors)
    rows = jnp.concatenate(parts, axis=0)
    k_ref[...] = rows[:, :HD]
    lane = lax.broadcasted_iota(jnp.int32, (1, 2 * KEEP), 1)
    row = lax.broadcasted_iota(jnp.int32, (16, 2 * KEEP), 0)
    for i in range(len(flags) // 2):
        cols = slice(i * 2 * KEEP, (i + 1) * 2 * KEEP)
        one = jnp.where(lane < KEEP, flags[2 * i].astype(F32), flags[2 * i + 1].astype(F32))
        vt_ref[:HD, cols] = (rows[cols, HD:].astype(F32).T * one).astype(BF)
        vt_ref[HD:, cols] = jnp.where(row == 0, one, 0.0).astype(BF)


def early_kernel(tags, q_ref, k_own, v_own, *refs):
    n = len(tags)
    payloads = refs[:n]
    state_ref, q_norm_ref, k_norm_ref, k_ref, vt_ref = refs[n:]
    step = pl.program_id(0)
    near = k_ref.shape[0]

    @pl.when(step == 0)
    def _():
        lay(tags, payloads, (), k_ref, vt_ref)
        vt_ref[:HD, near:] = v_own[...].astype(F32).T.astype(BF)
        rows = lax.broadcasted_iota(jnp.int32, (16, BLK), 0)
        vt_ref[HD:, near:] = jnp.where(rows == 0, 1.0, 0.0).astype(BF)
        q_norm_ref[...] = jnp.zeros_like(q_norm_ref)
        k_norm_ref[...] = jnp.maximum(norm2(k_own[...]), norm2(k_ref[...]))

    q = heads_below(q_ref[...])
    q_norm_ref[...] = jnp.maximum(q_norm_ref[...], norm2(q))
    key = lax.broadcasted_iota(jnp.int32, (ROWS, COLS), 0)
    token = lax.broadcasted_iota(jnp.int32, (ROWS, COLS), 1) % ROWS
    for chunk in range(BLK // ROWS):
        @pl.when(step == chunk)
        def _():
            full = chunk * ROWS
            weights = [jnp.exp2(dot_t(k_ref[...], q) * SCALE).astype(BF)]
            if full:
                weights.append(jnp.exp2(dot_t(k_own[:full, :], q) * SCALE).astype(BF))
            scores = dot_t(k_own[full:full + ROWS, :], q) * SCALE
            weights.append(jnp.where(key <= token, jnp.exp2(scores), 0.0).astype(BF))
            state_ref[0] = dot(vt_ref[:, :near + full + ROWS], jnp.concatenate(weights, axis=0))


def early(tags, queries, key_rows, value_rows, payloads):
    near = len(tags) * len(DZ) * KEEP
    cost = 4096 * (near + BLK) * HD
    return pl.pallas_call(
        functools.partial(early_kernel, tags),
        grid=(BLK // ROWS,),
        out_shape=(state_shape(), NORM, NORM),
        in_specs=[
            pl.BlockSpec((ROWS, GROUP * HD), lambda i: (i, 0)), same((BLK, HD)), same((BLK, HD)),
        ] + [same((PAY, 2 * HD))] * len(tags),
        out_specs=(STATE, same((8, HD)), same((8, HD))),
        scratch_shapes=[pltpu.VMEM((near, HD), BF), pltpu.VMEM((VROWS, near + BLK), BF)],
        compiler_params=params(),
        cost_estimate=pl.CostEstimate(flops=8 * cost, bytes_accessed=4 << 20, transcendentals=cost // HD),
        name="early",
    )(queries, key_rows, value_rows, *payloads)


def general(queries, k_own, v_own, payloads, out, q_ref, out_ref, stage, kv_own, peak_ref, total_ref, acc_ref, sem):
    copies = [pltpu.make_async_copy(k_own, kv_own.at[0], sem.at[0]), pltpu.make_async_copy(v_own, kv_own.at[1], sem.at[1])]
    copies += [pltpu.make_async_copy(ref, stage.at[i], sem.at[2 + i]) for i, ref in enumerate(payloads)]
    for copy in copies:
        copy.start()
    for copy in copies:
        copy.wait()
    me, z, x, core = place()

    def one_chunk(chunk, carry):
        rows = pl.ds(pl.multiple_of(chunk * ROWS, ROWS), ROWS)
        pltpu.sync_copy(queries.at[rows, :], q_ref)
        q = heads_below(q_ref[...])
        peak_ref[...] = jnp.full(peak_ref.shape, -1e30, F32)
        total_ref[...] = jnp.zeros(total_ref.shape, F32)
        acc_ref[...] = jnp.zeros(acc_ref.shape, F32)

        def take(keys, values, seen):
            scores = jnp.where(seen, dot_t(keys, q), -1e30)
            peak = peak_ref[0:1, :]
            new_peak = jnp.maximum(peak, jnp.max(scores, axis=0, keepdims=True))
            shrink = jnp.exp2((peak - new_peak) * SCALE)
            weights = jnp.where(seen, jnp.exp2((scores - new_peak) * SCALE), 0.0)
            peak_ref[0:1, :] = new_peak
            total_ref[0:1, :] = total_ref[0:1, :] * shrink + jnp.sum(weights, axis=0, keepdims=True)
            update = dot(values.astype(F32).T.astype(BF), weights.astype(BF))
            acc_ref[...] = acc_ref[...] * shrink + update

        token = chunk * ROWS + lax.broadcasted_iota(jnp.int32, (BLK, COLS), 1) % ROWS
        take(kv_own[0], kv_own[1], lax.broadcasted_iota(jnp.int32, (BLK, COLS), 0) <= token)
        row = lax.broadcasted_iota(jnp.int32, (PAY, COLS), 0) // KEEP

        def one(i, inner):
            base = ((x - i // CORES + X) % X) * CORES + (core + i % CORES) % CORES
            hosts = jnp.full((PAY, COLS), -1, jnp.int32)
            for b in range(len(DZ)):
                hosts = jnp.where(row == b, ((z - DZ[b] + Z) % Z) * (X * CORES) + base, hosts)
            rows = stage[i]
            take(rows[:, :HD], rows[:, HD:], hosts < me)
            return inner

        lax.fori_loop(0, jnp.where(me >= 1, X * CORES, 0), one, 0)
        result = acc_ref[...] / total_ref[0:1, :]
        for h in range(GROUP):
            out_ref[:, h * HD:(h + 1) * HD] = result[:, h * ROWS:(h + 1) * ROWS].T.astype(BF)
        pltpu.sync_copy(out_ref, out.at[rows, :])
        return carry

    lax.fori_loop(0, BLK // ROWS, one_chunk, 0)


def lay_kernel(tags, *refs):
    n, m = len(tags), len(tags) + X * CORES
    q_norm, norms, queries, k_own, v_own = refs[m:m + 5]
    k_ref, vt_ref, plain_ref, out, *scratch = refs[m + 5:]
    lay(tags, refs[:n], refs[n:m], k_ref, vt_ref)
    key_norm = jnp.maximum(norms[...], norm2(k_ref[...]))
    plain = (q_norm[...] * key_norm <= LIMIT).astype(F32)
    plain_ref[...] = plain

    @pl.when(plain[0, 0] <= 0.0)
    def _():
        general(queries, k_own, v_own, refs[n:m], out, *scratch)


def lay_out(tags, payloads, everything, norms, queries, key_rows, value_rows):
    keys = (len(tags) * len(DZ) + X * CORES) * KEEP
    return pl.pallas_call(
        functools.partial(lay_kernel, tags),
        out_shape=(
            jax.ShapeDtypeStruct((keys, HD), BF), jax.ShapeDtypeStruct((VROWS, keys), BF), NORM,
            jax.ShapeDtypeStruct(queries.shape, BF),
        ),
        in_specs=[VMEM] * (len(tags) + X * CORES + 2) + [ANY] * 3,
        out_specs=(VMEM, VMEM, VMEM, ANY),
        scratch_shapes=[
            pltpu.VMEM((ROWS, GROUP * HD), BF), pltpu.VMEM((ROWS, GROUP * HD), BF),
            pltpu.VMEM((X * CORES, PAY, 2 * HD), BF), pltpu.VMEM((2, BLK, HD), BF),
            pltpu.VMEM((8, COLS), F32), pltpu.VMEM((8, COLS), F32), pltpu.VMEM((HD, COLS), F32),
            pltpu.SemaphoreType.DMA((2 + X * CORES,)),
        ],
        compiler_params=params(),
        name="lay",
    )(*payloads, *everything, *norms, queries, key_rows, value_rows)


def chunk_of(off):
    return (lax.axis_index("tp") + off) % (BLK // ROWS)


def final_kernel(off, q_ref, state_in, k_ref, vt_ref, plain_ref, general_out, *rest):
    out_ref = rest[-1]
    plain = plain_ref[0, 0] > 0.0
    chunk = chunk_of(off)
    rows = pl.ds(pl.multiple_of(chunk * ROWS, ROWS), ROWS)

    @pl.when(plain)
    def _():
        weights = jnp.exp2(dot_t(k_ref[...], heads_below(q_ref[rows, :])) * SCALE).astype(BF)
        total = state_in[chunk] + dot(vt_ref[...], weights)
        result = total[:HD] / total[HD:HD + 1]
        for h in range(GROUP):
            out_ref[:, h * HD:(h + 1) * HD] = result[:, h * ROWS:(h + 1) * ROWS].T.astype(BF)

    @pl.when(jnp.logical_not(plain))
    def _():
        pltpu.sync_copy(general_out.at[rows, :], out_ref)


def final(off, queries, state, keys, values, plain, general_out, others):
    count = keys.shape[0]
    return pl.pallas_call(
        functools.partial(final_kernel, off),
        in_specs=[VMEM, VMEM, VMEM, VMEM, VMEM, ANY] + [ANY] * len(others),
        out_specs=VMEM,
        out_shape=jax.ShapeDtypeStruct((ROWS, GROUP * HD), BF),
        compiler_params=params(),
        cost_estimate=pl.CostEstimate(flops=2 * 2 * 1024 * count * 128 * 2, bytes_accessed=2 << 20, transcendentals=1024 * count),
        name="final",
    )(queries, state, keys, values, plain, general_out, *others)


def join_kernel(order, *refs):
    parts, out_ref, sem = refs[:-2], refs[-2], refs[-1]
    y = lax.axis_index("tp")
    width = GROUP * HD
    copies = []
    for i, part in enumerate(parts):
        first = pl.multiple_of((y - order[i] + len(parts)) % len(parts) * width, width)
        copies.append(pltpu.make_async_copy(part, out_ref.at[:, pl.ds(first, width)], sem.at[i]))
    for copy in copies:
        copy.start()
    for copy in copies:
        copy.wait()


def join(order, parts):
    return pl.pallas_call(
        functools.partial(join_kernel, order),
        out_shape=jax.ShapeDtypeStruct((ROWS, len(parts) * GROUP * HD), BF),
        in_specs=[ANY] * len(parts),
        out_specs=ANY,
        scratch_shapes=[pltpu.SemaphoreType.DMA((len(parts),))],
        compiler_params=params(),
        name="join",
    )(*parts)


def host_of(z, x, core):
    return ((z % Z) * X + x % X) * CORES + core % CORES


ALL = [(z, x, c) for z in range(Z) for x in range(X) for c in range(CORES)]


def move(value, dz=0, dx=0, dcore=0):
    pairs = [(host_of(z, x, c), host_of(z + dz, x + dx, c + dcore)) for z, x, c in ALL]
    return lax.ppermute(value, "ctx", pairs)


def body(queries, key_rows, value_rows, keep_rows):
    me, z, x, core = place()
    passing, *pieces = select(keep_rows, key_rows, value_rows)

    pair = [pieces[0]] + [move(pieces[dx], dx=dx) for dx in (1, 2, 3)]
    pair = functools.reduce(lambda a, dx: jnp.where(x == dx, pair[dx], a), (1, 2, 3), pair[0])
    piece = jnp.where(core == 0, pair[:KEEP], move(pair[KEEP:], dcore=1))

    here = jnp.concatenate([passing, piece], axis=0)
    planes = {0: here}
    for dz in (2, -2, 1, -1):
        planes[dz] = move(here, dz=dz)
    planes[4] = move(planes[-2], dz=-2)
    planes[3] = move(planes[2], dz=1)
    planes[-3] = move(planes[-2], dz=-1)
    anchor = piece
    for dz, plane in planes.items():
        if dz:
            anchor = jnp.where(z == dz % Z, plane[KEEP:], anchor)
    payload = jnp.concatenate([planes[dz][:KEEP] for dz in DZ] + [anchor], axis=0)

    across = {0: payload}
    for dx in (1, 3, 2):
        across[dx] = move(payload, dx=dx)
    other = {0: move(across[0], dcore=1)}
    state, q_norm, k_norm = early([(0, 0), (0, 1)], queries, key_rows, value_rows, [across[0], other[0]])
    across[1], across[3], across[2], state = lax.optimization_barrier((across[1], across[3], across[2], state))
    for dx in (1, 3, 2):
        other[dx] = move(across[dx], dcore=1)
    everything = [v[dx] for dx in range(X) for v in (across, other)]

    tags = [(dx, dc) for dx in (1, 3, 2) for dc in (0, 1)]
    payloads = [v[dx] for dx in (1, 3, 2) for v in (across, other)]
    keys, values, plain, general_out = lay_out(
        tags, payloads, everything, [q_norm, k_norm], queries, key_rows, value_rows)

    ranks = lax.axis_size("tp")
    parts = {}
    order = (0, 2, 1, 3)
    for off in order:
        part = final(off, queries, state, keys, values, plain, general_out, everything)
        if off:
            part = lax.ppermute(part, "tp", [(i, (i + off) % ranks) for i in range(ranks)])
        parts[off] = part
    return join(order, [parts[off] for off in order])


def solution(mesh):
    in_specs = (P("ctx", "tp"), P("ctx", "tp"), P("ctx", "tp"), P("ctx", None))
    out_specs = P(("ctx", "tp"), None)
    return jax.shard_map(body, mesh=mesh, in_specs=in_specs, out_specs=out_specs, check_vma=False)
```

```python
import functools

import jax
import jax.numpy as jnp
from jax import lax
from jax.experimental import pallas as pl
from jax.experimental.pallas import tpu as pltpu
from jax.sharding import PartitionSpec as P

BF = jnp.bfloat16
F32 = jnp.float32
Z, X, CORES = 8, 4, 2
HD, GROUP, KEEP, BLK = 128, 8, 64, 512
VROWS = HD + 16
DZ = (0, 1, -1, 2, -2, 3, -3, 4)
PAY = (len(DZ) + 1) * KEEP
LOG2E = 1.4426950408889634
SCALE = HD ** (-0.5) * LOG2E
LIMIT = 75.0 * 75.0 * HD
ROWS = 128
COLS = ROWS * GROUP
VMEM = pl.BlockSpec(memory_space=pltpu.VMEM)
ANY = pl.BlockSpec(memory_space=pl.ANY)
NORM = jax.ShapeDtypeStruct((8, HD), F32)


def params(mib=36):
    return pltpu.CompilerParams(vmem_limit_bytes=mib << 20)


def dot_t(a, b):
    return lax.dot_general(a, b, (((1,), (1,)), ((), ())), preferred_element_type=F32)


def dot(a, b):
    return lax.dot_general(a, b, (((1,), (0,)), ((), ())), preferred_element_type=F32)


def norm2(rows):
    rows = rows.astype(F32)
    most = jnp.max(jnp.sum(rows * rows, axis=1, keepdims=True), axis=0, keepdims=True)
    return jnp.broadcast_to(most, (8, HD))


def place():
    me = lax.axis_index("ctx")
    return me, me // (X * CORES), (me // CORES) % X, me % CORES


def origin_visible(dx, dcore, block):
    me, z, x, core = place()
    if block == len(DZ):
        return me >= 1
    host = ((z - DZ[block] + Z) % Z) * (X * CORES) + ((x - dx + X) % X) * CORES + (core + dcore) % CORES
    return host < me


def select_kernel(keep_ref, k_ref, v_ref, pass_ref, *piece_refs):
    chosen = (lax.broadcasted_iota(jnp.int32, (BLK, KEEP), 0) == keep_ref[...]).astype(BF)
    for side, ref in ((0, k_ref), (1, v_ref)):
        lanes = slice(side * HD, (side + 1) * HD)
        pass_ref[:, lanes] = lax.dot_general(
            chosen, ref[...], (((0,), (0,)), ((), ())), preferred_element_type=F32
        ).astype(BF)
        for x, piece_ref in enumerate(piece_refs):
            piece_ref[:, lanes] = ref[x * 2 * KEEP:(x + 1) * 2 * KEEP, :]


def same(shape):
    return pl.BlockSpec(shape, lambda *i: (0,) * len(shape))


def select(keep_rows, key_rows, value_rows):
    rows = [KEEP] + [2 * KEEP] * X
    return pl.pallas_call(
        select_kernel,
        grid=(1,),
        out_shape=tuple(jax.ShapeDtypeStruct((n, 2 * HD), BF) for n in rows),
        in_specs=[same((1, KEEP)), same((BLK, HD)), same((BLK, HD))],
        out_specs=tuple(same((n, 2 * HD)) for n in rows),
        compiler_params=params(),
        name="select",
    )(keep_rows, key_rows, value_rows)


def heads_below(q):
    return jnp.concatenate([q[:, h * HD:(h + 1) * HD] for h in range(q.shape[1] // HD)], axis=0)


def state_shape():
    return jax.ShapeDtypeStruct((BLK // ROWS, VROWS, COLS), F32)


STATE = pl.BlockSpec((1, VROWS, COLS), lambda i: (i, 0, 0))


def lay(tags, payload_refs, anchors, k_ref, vt_ref):
    blocks = len(DZ)
    own_rows = blocks * KEEP
    parts = [ref[:own_rows, :] for ref in payload_refs]
    flags = [origin_visible(dx, dcore, b) for dx, dcore in tags for b in range(blocks)]
    if anchors:
        parts += [ref[own_rows:, :] for ref in anchors]
        flags += [lax.axis_index("ctx") >= 1] * len(anchors)
    rows = jnp.concatenate(parts, axis=0)
    k_ref[...] = rows[:, :HD]
    lane = lax.broadcasted_iota(jnp.int32, (1, 2 * KEEP), 1)
    row = lax.broadcasted_iota(jnp.int32, (16, 2 * KEEP), 0)
    for i in range(len(flags) // 2):
        cols = slice(i * 2 * KEEP, (i + 1) * 2 * KEEP)
        one = jnp.where(lane < KEEP, flags[2 * i].astype(F32), flags[2 * i + 1].astype(F32))
        vt_ref[:HD, cols] = (rows[cols, HD:].astype(F32).T * one).astype(BF)
        vt_ref[HD:, cols] = jnp.where(row == 0, one, 0.0).astype(BF)


def early_kernel(tags, q_ref, k_own, v_own, *refs):
    n = len(tags)
    payloads = refs[:n]
    state_ref, q_norm_ref, k_norm_ref, k_ref, vt_ref = refs[n:]
    step = pl.program_id(0)
    near = k_ref.shape[0]

    @pl.when(step == 0)
    def _():
        lay(tags, payloads, (), k_ref, vt_ref)
        vt_ref[:HD, near:] = v_own[...].astype(F32).T.astype(BF)
        rows = lax.broadcasted_iota(jnp.int32, (16, BLK), 0)
        vt_ref[HD:, near:] = jnp.where(rows == 0, 1.0, 0.0).astype(BF)
        q_norm_ref[...] = jnp.zeros_like(q_norm_ref)
        k_norm_ref[...] = jnp.maximum(norm2(k_own[...]), norm2(k_ref[...]))

    q = heads_below(q_ref[...])
    q_norm_ref[...] = jnp.maximum(q_norm_ref[...], norm2(q))
    key = lax.broadcasted_iota(jnp.int32, (ROWS, COLS), 0)
    token = lax.broadcasted_iota(jnp.int32, (ROWS, COLS), 1) % ROWS
    for chunk in range(BLK // ROWS):
        @pl.when(step == chunk)
        def _():
            full = chunk * ROWS
            weights = [jnp.exp2(dot_t(k_ref[...], q) * SCALE).astype(BF)]
            if full:
                weights.append(jnp.exp2(dot_t(k_own[:full, :], q) * SCALE).astype(BF))
            scores = dot_t(k_own[full:full + ROWS, :], q) * SCALE
            weights.append(jnp.where(key <= token, jnp.exp2(scores), 0.0).astype(BF))
            state_ref[0] = dot(vt_ref[:, :near + full + ROWS], jnp.concatenate(weights, axis=0))


def early(tags, queries, key_rows, value_rows, payloads):
    near = len(tags) * len(DZ) * KEEP
    cost = 4096 * (near + BLK) * HD
    return pl.pallas_call(
        functools.partial(early_kernel, tags),
        grid=(BLK // ROWS,),
        out_shape=(state_shape(), NORM, NORM),
        in_specs=[
            pl.BlockSpec((ROWS, GROUP * HD), lambda i: (i, 0)), same((BLK, HD)), same((BLK, HD)),
        ] + [same((PAY, 2 * HD))] * len(tags),
        out_specs=(STATE, same((8, HD)), same((8, HD))),
        scratch_shapes=[pltpu.VMEM((near, HD), BF), pltpu.VMEM((VROWS, near + BLK), BF)],
        compiler_params=params(),
        cost_estimate=pl.CostEstimate(flops=8 * cost, bytes_accessed=4 << 20, transcendentals=cost // HD),
        name="early",
    )(queries, key_rows, value_rows, *payloads)


def general(queries, k_own, v_own, payloads, out, q_ref, out_ref, stage, kv_own, peak_ref, total_ref, acc_ref, sem):
    copies = [pltpu.make_async_copy(k_own, kv_own.at[0], sem.at[0]), pltpu.make_async_copy(v_own, kv_own.at[1], sem.at[1])]
    copies += [pltpu.make_async_copy(ref, stage.at[i], sem.at[2 + i]) for i, ref in enumerate(payloads)]
    for copy in copies:
        copy.start()
    for copy in copies:
        copy.wait()
    me, z, x, core = place()

    def one_chunk(chunk, carry):
        rows = pl.ds(pl.multiple_of(chunk * ROWS, ROWS), ROWS)
        pltpu.sync_copy(queries.at[rows, :], q_ref)
        q = heads_below(q_ref[...])
        peak_ref[...] = jnp.full(peak_ref.shape, -1e30, F32)
        total_ref[...] = jnp.zeros(total_ref.shape, F32)
        acc_ref[...] = jnp.zeros(acc_ref.shape, F32)

        def take(keys, values, seen):
            scores = jnp.where(seen, dot_t(keys, q), -1e30)
            peak = peak_ref[0:1, :]
            new_peak = jnp.maximum(peak, jnp.max(scores, axis=0, keepdims=True))
            shrink = jnp.exp2((peak - new_peak) * SCALE)
            weights = jnp.where(seen, jnp.exp2((scores - new_peak) * SCALE), 0.0)
            peak_ref[0:1, :] = new_peak
            total_ref[0:1, :] = total_ref[0:1, :] * shrink + jnp.sum(weights, axis=0, keepdims=True)
            update = dot(values.astype(F32).T.astype(BF), weights.astype(BF))
            acc_ref[...] = acc_ref[...] * shrink + update

        token = chunk * ROWS + lax.broadcasted_iota(jnp.int32, (BLK, COLS), 1) % ROWS
        take(kv_own[0], kv_own[1], lax.broadcasted_iota(jnp.int32, (BLK, COLS), 0) <= token)
        row = lax.broadcasted_iota(jnp.int32, (PAY, COLS), 0) // KEEP

        def one(i, inner):
            base = ((x - i // CORES + X) % X) * CORES + (core + i % CORES) % CORES
            hosts = jnp.full((PAY, COLS), -1, jnp.int32)
            for b in range(len(DZ)):
                hosts = jnp.where(row == b, ((z - DZ[b] + Z) % Z) * (X * CORES) + base, hosts)
            rows = stage[i]
            take(rows[:, :HD], rows[:, HD:], hosts < me)
            return inner

        lax.fori_loop(0, jnp.where(me >= 1, X * CORES, 0), one, 0)
        result = acc_ref[...] / total_ref[0:1, :]
        for h in range(GROUP):
            out_ref[:, h * HD:(h + 1) * HD] = result[:, h * ROWS:(h + 1) * ROWS].T.astype(BF)
        pltpu.sync_copy(out_ref, out.at[rows, :])
        return carry

    lax.fori_loop(0, BLK // ROWS, one_chunk, 0)


def lay_kernel(tags, *refs):
    n, m = len(tags), len(tags) + X * CORES
    q_norm, norms, queries, k_own, v_own = refs[m:m + 5]
    k_ref, vt_ref, plain_ref, out, *scratch = refs[m + 5:]
    lay(tags, refs[:n], refs[n:m], k_ref, vt_ref)
    key_norm = jnp.maximum(norms[...], norm2(k_ref[...]))
    plain = (q_norm[...] * key_norm <= LIMIT).astype(F32)
    plain_ref[...] = plain

    @pl.when(plain[0, 0] <= 0.0)
    def _():
        general(queries, k_own, v_own, refs[n:m], out, *scratch)


def lay_out(tags, payloads, everything, norms, queries, key_rows, value_rows):
    keys = (len(tags) * len(DZ) + X * CORES) * KEEP
    return pl.pallas_call(
        functools.partial(lay_kernel, tags),
        out_shape=(
            jax.ShapeDtypeStruct((keys, HD), BF), jax.ShapeDtypeStruct((VROWS, keys), BF), NORM,
            jax.ShapeDtypeStruct(queries.shape, BF),
        ),
        in_specs=[VMEM] * (len(tags) + X * CORES + 2) + [ANY] * 3,
        out_specs=(VMEM, VMEM, VMEM, ANY),
        scratch_shapes=[
            pltpu.VMEM((ROWS, GROUP * HD), BF), pltpu.VMEM((ROWS, GROUP * HD), BF),
            pltpu.VMEM((X * CORES, PAY, 2 * HD), BF), pltpu.VMEM((2, BLK, HD), BF),
            pltpu.VMEM((8, COLS), F32), pltpu.VMEM((8, COLS), F32), pltpu.VMEM((HD, COLS), F32),
            pltpu.SemaphoreType.DMA((2 + X * CORES,)),
        ],
        compiler_params=params(),
        name="lay",
    )(*payloads, *everything, *norms, queries, key_rows, value_rows)


def chunk_of(off):
    return (lax.axis_index("tp") + off) % (BLK // ROWS)


def final_kernel(off, q_ref, state_in, k_ref, vt_ref, plain_ref, general_out, *rest):
    out_ref = rest[-1]
    plain = plain_ref[0, 0] > 0.0
    chunk = chunk_of(off)
    rows = pl.ds(pl.multiple_of(chunk * ROWS, ROWS), ROWS)

    @pl.when(plain)
    def _():
        weights = jnp.exp2(dot_t(k_ref[...], heads_below(q_ref[rows, :])) * SCALE).astype(BF)
        total = state_in[chunk] + dot(vt_ref[...], weights)
        result = total[:HD] / total[HD:HD + 1]
        for h in range(GROUP):
            out_ref[:, h * HD:(h + 1) * HD] = result[:, h * ROWS:(h + 1) * ROWS].T.astype(BF)

    @pl.when(jnp.logical_not(plain))
    def _():
        pltpu.sync_copy(general_out.at[rows, :], out_ref)


def final(off, queries, state, keys, values, plain, general_out, others):
    count = keys.shape[0]
    return pl.pallas_call(
        functools.partial(final_kernel, off),
        in_specs=[VMEM, VMEM, VMEM, VMEM, VMEM, ANY] + [ANY] * len(others),
        out_specs=VMEM,
        out_shape=jax.ShapeDtypeStruct((ROWS, GROUP * HD), BF),
        compiler_params=params(),
        cost_estimate=pl.CostEstimate(flops=2 * 2 * 1024 * count * 128 * 2, bytes_accessed=2 << 20, transcendentals=1024 * count),
        name="final",
    )(queries, state, keys, values, plain, general_out, *others)


def join_kernel(order, *refs):
    parts, out_ref, sem = refs[:-2], refs[-2], refs[-1]
    y = lax.axis_index("tp")
    width = GROUP * HD
    copies = []
    for i, part in enumerate(parts):
        first = pl.multiple_of((y - order[i] + len(parts)) % len(parts) * width, width)
        copies.append(pltpu.make_async_copy(part, out_ref.at[:, pl.ds(first, width)], sem.at[i]))
    for copy in copies:
        copy.start()
    for copy in copies:
        copy.wait()


def join(order, parts):
    return pl.pallas_call(
        functools.partial(join_kernel, order),
        out_shape=jax.ShapeDtypeStruct((ROWS, len(parts) * GROUP * HD), BF),
        in_specs=[ANY] * len(parts),
        out_specs=ANY,
        scratch_shapes=[pltpu.SemaphoreType.DMA((len(parts),))],
        compiler_params=params(),
        name="join",
    )(*parts)


def host_of(z, x, core):
    return ((z % Z) * X + x % X) * CORES + core % CORES


ALL = [(z, x, c) for z in range(Z) for x in range(X) for c in range(CORES)]


def move(value, dz=0, dx=0, dcore=0):
    pairs = [(host_of(z, x, c), host_of(z + dz, x + dx, c + dcore)) for z, x, c in ALL]
    return lax.ppermute(value, "ctx", pairs)


def body(queries, key_rows, value_rows, keep_rows):
    me, z, x, core = place()
    passing, *pieces = select(keep_rows, key_rows, value_rows)

    pair = [pieces[0]] + [move(pieces[dx], dx=dx) for dx in (1, 2, 3)]
    pair = functools.reduce(lambda a, dx: jnp.where(x == dx, pair[dx], a), (1, 2, 3), pair[0])
    piece = jnp.where(core == 0, pair[:KEEP], move(pair[KEEP:], dcore=1))

    here = jnp.concatenate([passing, piece], axis=0)
    planes = {0: here}
    for dz in (2, -2, 1, -1):
        planes[dz] = move(here, dz=dz)
    planes[4] = move(planes[-2], dz=-2)
    planes[3] = move(planes[2], dz=1)
    planes[-3] = move(planes[-2], dz=-1)
    anchor = piece
    for dz, plane in planes.items():
        if dz:
            anchor = jnp.where(z == dz % Z, plane[KEEP:], anchor)
    payload = jnp.concatenate([planes[dz][:KEEP] for dz in DZ] + [anchor], axis=0)

    across = {0: payload}
    for dx in (1, 3, 2):
        across[dx] = move(payload, dx=dx)
    other = {0: move(across[0], dcore=1)}
    state, q_norm, k_norm = early([(0, 0), (0, 1)], queries, key_rows, value_rows, [across[0], other[0]])
    for dx in (2, 3, 1):
        across[dx], state = lax.optimization_barrier((across[dx], state))
        other[dx] = move(across[dx], dcore=1)
    everything = [v[dx] for dx in range(X) for v in (across, other)]

    tags = [(dx, dc) for dx in (1, 3, 2) for dc in (0, 1)]
    payloads = [v[dx] for dx in (1, 3, 2) for v in (across, other)]
    keys, values, plain, general_out = lay_out(
        tags, payloads, everything, [q_norm, k_norm], queries, key_rows, value_rows)

    ranks = lax.axis_size("tp")
    parts = {}
    order = (0, 2, 1, 3)
    for off in order:
        part = final(off, queries, state, keys, values, plain, general_out, everything)
        if off:
            part = lax.ppermute(part, "tp", [(i, (i + off) % ranks) for i in range(ranks)])
        parts[off] = part
    return join(order, [parts[off] for off in order])


def solution(mesh):
    in_specs = (P("ctx", "tp"), P("ctx", "tp"), P("ctx", "tp"), P("ctx", None))
    out_specs = P(("ctx", "tp"), None)
    return jax.shard_map(body, mesh=mesh, in_specs=in_specs, out_specs=out_specs, check_vma=False)
```
